32 devices in a mesh: groups: 2 (over x), frame: 16 (over z, y, core).
Axes of the slice: x: 2, y: 2, z: 4, core: 2. Of those that a mesh axis runs over, the one named last changes fastest.
Arguments:
- query_in: bfloat16 [32, 512, 1536], P(('groups', 'frame')), parts along dimension 0, may hold values from -200 to 200, as said below
- keys_in: bfloat16 [32, 512, 1536], P(('groups', 'frame')), parts along dimension 0, may hold values from -7 to 7, as said below
- values_in: bfloat16 [32, 512, 1536], P(('groups', 'frame')), parts along dimension 0, may hold values from -6 to 6
- far_picks: int32 [32, 6], P('groups'), parts along dimension 0, may hold values from 0 to 3
- win_rows: int32 [32], P(('groups', 'frame')), parts along dimension 0, may hold values from 1 to 15, as said below
Outputs:
- attended: bfloat16 [32, 512, 1536], P(('groups', 'frame')), parts along dimension 0
The draws below stay inside these ranges and needn't reach their ends.
There are 2 independent parts, one for each index of `groups`. The reference program is written for one: setup_inputs(seed, part) draws one part's arguments, and reference() takes and returns one part's arrays. A program takes and returns all parts, laid end to end along the dimension named above; each array names one. Nothing has to cross between parts.
Inputs may be any that keep to these rules, and one draw needn't show every extreme that they name: `query_in`: entries of the queries lie within this range. `keys_in`: entries of the keys lie within this range. `win_rows`: every draw has a frame with window 1 and a frame with window 16 - 1.
All inputs are finite; a program needn't handle non-finite values.
Results may differ from the reference program's by a relative error of at most 0.0032.
Values may be sent and summed in bfloat16 or wider, within the bound.
A program may use at most 128 MiB of HBM per device.

```python
import math
import jax
import jax.numpy as jnp
from jax import lax

HD = 128
ROWS = 16
COLS = 32
SUB = 128
NREACH = 3
WIDTH = 1536
TOK = 512
FRAMES = 16
NFAR = 6


def paired_fields(key):
    first_key = jax.random.fold_in(key, 11)
    second_key = jax.random.fold_in(key, 12)
    shape = (FRAMES, TOK, WIDTH)
    keys_field = jax.random.truncated_normal(first_key, -6.0, 6.0, shape, jnp.float32)
    query_field = 2.5 * jax.random.truncated_normal(second_key, -6.0, 6.0, shape, jnp.float32)
    return (query_field, keys_field)


def draw_query_in(key, part):
    return paired_fields(key)[0].astype(jnp.bfloat16)


def draw_keys_in(key, part):
    return paired_fields(key)[1].astype(jnp.bfloat16)


def draw_win_rows(key, part):
    first_key = jax.random.fold_in(key, 21)
    second_key = jax.random.fold_in(key, 22)
    third_key = jax.random.fold_in(key, 23)
    windows = jax.random.randint(first_key, (FRAMES,), 1, ROWS, jnp.int32)
    low_spot = jax.random.randint(second_key, (), 0, FRAMES, jnp.int32)
    high_spot = (low_spot + 1 + jax.random.randint(third_key, (), 0, FRAMES - 1, jnp.int32)) % FRAMES
    windows = windows.at[low_spot].set(1)
    windows = windows.at[high_spot].set(ROWS - 1)
    return windows


def plant(values, rng, low, top_value):
    longest = values.shape.index(max(values.shape))
    spots = []
    for shift in (0, 1):
        where = [jax.random.randint(jax.random.fold_in(rng, axis), (), 0, length) for axis, length in enumerate(values.shape)]
        where[longest] = (where[longest] + shift) % values.shape[longest]
        spots.append(tuple(where))
    return values.at[spots[0]].set(low).at[spots[1]].set(top_value)


def levels(key, shape, pieces, least, top_value):
    gain, own = 1.0, jax.random.fold_in(key, 6)
    for dim, parts in pieces:
        heights = jnp.exp(jax.random.uniform(jax.random.fold_in(own, dim), (parts,), jnp.float32, least / len(pieces), top_value / len(pieces)))
        gain = gain * jnp.repeat(heights, shape[dim] // parts).reshape([-1 if axis == dim else 1 for axis in range(len(shape))])
    return gain


def noise(own_key, extent, width, bound, split=(), kind=jnp.bfloat16):
    drawn = width * jax.random.normal(own_key, extent, jnp.float32)
    if split:
        drawn = drawn * levels(own_key, extent, split, -0.22, 0.18)
    return jnp.clip(drawn, -bound, bound).astype(kind)


def setup_inputs(seed: int = 0, part: int = 0) -> dict:
    key_list = jax.random.split(jax.random.key(seed), 6)
    own_keys = jax.random.split(jax.random.fold_in(key_list[5], part), 6)
    return {
        "query_in": draw_query_in(jax.random.fold_in(jax.random.fold_in(key_list[5], part), 71), part),
        "keys_in": draw_keys_in(jax.random.fold_in(jax.random.fold_in(key_list[5], part), 71), part),
        "values_in": noise(own_keys[2], (FRAMES, TOK, WIDTH), 1.0, 6.0, ((0, 16),)),
        "far_picks": plant(jax.random.randint(own_keys[3], (FRAMES, NFAR), 0, TOK // SUB), jax.random.fold_in(own_keys[3], 1), 0, (TOK // SUB) - 1).astype(jnp.int32),
        "win_rows": draw_win_rows(jax.random.fold_in(jax.random.fold_in(key_list[5], part), 71), part),
    }


def offsets_for(frames):
    spacing = [frames // 2 ** (NREACH - level_index) for level_index in range(NREACH)]
    return [-stride for stride in spacing] + [stride for stride in spacing]

def build_mask(window, frame_ok, far_ok, tokens_count):
    query_rows = jnp.arange(tokens_count, dtype=jnp.int32) // COLS
    key_rows = jnp.tile(query_rows, 3)
    nearby = jnp.abs(query_rows[:, None] - key_rows[None, :]) <= window
    nearby = nearby & jnp.repeat(frame_ok, tokens_count)[None, :]
    distant = jnp.repeat(far_ok, SUB)[None, :]
    distant = jnp.broadcast_to(distant, (tokens_count, distant.shape[1]))
    return jnp.concatenate([nearby, distant], axis=1)

def attend(queries, key_value, allowed):
    tokens_count = queries.shape[0]
    model_width = queries.shape[1]
    heads_count = model_width // HD

    def split_heads(matrix):
        return matrix.reshape(matrix.shape[0], heads_count, HD).transpose(1, 0, 2)
    query_heads = split_heads(queries)
    key_heads = split_heads(key_value[:, :model_width])
    value_heads = split_heads(key_value[:, model_width:])

    def one_head(operands):
        query_head, key_head, value_head = operands
        scores = lax.dot_general(query_head, key_head, (((1,), (1,)), ((), ())), preferred_element_type=jnp.float32)
        scores = scores * (1.0 / math.sqrt(HD))
        scores = jnp.where(allowed, scores, -1e+30)
        row_peak = lax.optimization_barrier(jnp.max(scores, axis=1, keepdims=True))
        raw_weights = jnp.exp(scores - row_peak)
        row_total = lax.optimization_barrier(jnp.sum(raw_weights, axis=1, keepdims=True))
        weighted = jnp.dot(raw_weights.astype(jnp.bfloat16), value_head, preferred_element_type=jnp.float32)
        return weighted / row_total
    heads_out = lax.map(one_head, (query_heads, key_heads, value_heads))
    return heads_out.transpose(1, 0, 2).reshape(tokens_count, model_width).astype(jnp.bfloat16)

def reference(query_in, keys_in, values_in, far_picks, win_rows):
    key_value = jnp.concatenate([keys_in, values_in], axis=2)
    tokens_count = key_value.shape[1]
    double_width = key_value.shape[2]
    padded = jnp.pad(key_value, ((1, 1), (0, 0), (0, 0)))
    offset_list = jnp.array(offsets_for(FRAMES), dtype=jnp.int32)

    def one_frame(position):
        beside_all = lax.dynamic_slice_in_dim(padded, position, 3, 0).reshape(3 * tokens_count, double_width)
        sources = jnp.clip(position + offset_list, 0, FRAMES - 1).astype(jnp.int32)
        picks_row = far_picks[position].astype(jnp.int32)

        def take_block(source, picked):
            start = (picked * SUB).astype(jnp.int32)
            return lax.dynamic_slice(key_value, (source, start, jnp.int32(0)), (1, SUB, double_width))[0]
        distant = jax.vmap(take_block)(sources, picks_row).reshape(offset_list.shape[0] * SUB, double_width)
        frame_ok = jnp.stack([position >= 1, position >= 0, position + 1 < FRAMES])
        far_ok = (position + offset_list >= 0) & (position + offset_list < FRAMES)
        allowed = build_mask(win_rows[position], frame_ok, far_ok, tokens_count)
        key_all = jnp.concatenate([beside_all, distant], axis=0)
        return attend(query_in[position], key_all, allowed)
    return lax.map(one_frame, jnp.arange(FRAMES, dtype=jnp.int32))
```

```python
import functools
import math

import jax
import jax.numpy as jnp
from jax import lax
from jax.experimental import pallas as pl
from jax.experimental.pallas import tpu as pltpu
from jax.sharding import PartitionSpec as P

HD = 128
COLS = 32
SUB = 128
NREACH = 3
NEG = -1e30
CHUNKS = 3
TILE = 256
FACTOR = math.log2(math.e) / math.sqrt(HD)


def kernel(
    frames, q_hbm, k_hbm, v_hbm, picks, win, out_ref,
    qs, ks, vs, near_k, near_v, stage_k, stage_v, far_k, far_v,
    peak, total, acc, bias,
    in_sem, near_send, near_recv, far_send, far_recv,
):
    tokens, width = qs.shape
    heads = width // HD
    part = width // CHUNKS
    part_heads = heads // CHUNKS
    group = lax.axis_index("groups")
    me = lax.axis_index("frame")
    steps = [frames // 2 ** (NREACH - j) for j in range(NREACH)]

    def device(index):
        return (group, index)

    far_offsets = [-steps[0], steps[0], -steps[1], steps[1]]

    def inside(index):
        return (index >= 0) & (index < frames)

    partners = [-1, 1] + far_offsets + [-steps[2], steps[2]]

    loads = [
        pltpu.make_async_copy(src, dst, in_sem.at[i])
        for i, (src, dst) in enumerate(((k_hbm.at[0], ks), (v_hbm.at[0], vs), (q_hbm.at[0], qs)))
    ]
    for load in loads:
        load.start()

    barrier = pltpu.get_barrier_semaphore()
    count = jnp.int32(0)
    for offset in partners:
        ok = inside(me + offset)
        count = count + ok.astype(jnp.int32)

        @pl.when(ok)
        def _():
            pl.semaphore_signal(
                barrier, inc=1, device_id=device(me + offset), device_id_type=pl.DeviceIdType.MESH
            )
    pl.semaphore_wait(barrier, count)

    def near_copy(side, chunk, kind):
        target = me + 1 if side == 0 else me - 1
        src = (k_hbm, v_hbm)[kind].at[0, :, pl.ds(chunk * part, part)]
        dst = (near_k, near_v)[kind].at[side, :, pl.ds(chunk * part, part)]
        return pltpu.make_async_remote_copy(
            src_ref=src, dst_ref=dst,
            send_sem=near_send.at[side, chunk, kind], recv_sem=near_recv.at[side, chunk, kind],
            device_id=device(target), device_id_type=pl.DeviceIdType.MESH,
        )

    def each_near(action):
        for chunk in range(CHUNKS):
            for side in range(2):
                @pl.when(inside(me + 1 if side == 0 else me - 1))
                def _():
                    for kind in range(2):
                        action(near_copy(side, chunk, kind))

    each_near(lambda copy: copy.start())

    loads[0].wait()
    loads[1].wait()

    def far_copy(slot, offset, kind):
        rows = pl.ds(slot * SUB, SUB)
        return pltpu.make_async_remote_copy(
            src_ref=(stage_k, stage_v)[kind].at[rows, :], dst_ref=(far_k, far_v)[kind].at[rows, :],
            send_sem=far_send.at[slot, kind], recv_sem=far_recv.at[slot, kind],
            device_id=device(me - offset), device_id_type=pl.DeviceIdType.MESH,
        )

    long_slot = len(far_offsets)

    def stage(slot, pick):
        chosen = jnp.broadcast_to(pick, (16, HD))
        hot = [
            jnp.concatenate(
                [jnp.where(chosen == block, 1.0, 0.0).astype(stage_k.dtype)] * (SUB // 16), axis=0
            )
            for block in range(tokens // SUB)
        ]

        def one_head(head, carry):
            columns = pl.ds(pl.multiple_of(head * HD, HD), HD)
            for src, dst in ((ks, stage_k), (vs, stage_v)):
                mixed = hot[0] * src[pl.ds(0, SUB), columns]
                for block in range(1, tokens // SUB):
                    mixed = mixed + hot[block] * src[pl.ds(block * SUB, SUB), columns]
                dst[pl.ds(slot * SUB, SUB), columns] = mixed
            return carry
        lax.fori_loop(0, heads, one_head, 0)
    sends = [
        (long_slot, -steps[2], NREACH - 1), (long_slot, steps[2], 2 * NREACH - 1),
        (2, -steps[1], 1), (3, steps[1], NREACH + 1),
        (0, -steps[0], 0), (1, steps[0], NREACH),
    ]
    for slot, offset, column in sends:
        @pl.when(inside(me - offset))
        def _():
            stage(slot, picks[me - offset, column])
            far_copy(slot, offset, 0).start()
            far_copy(slot, offset, 1).start()

    for slot, offset in enumerate(far_offsets):
        @pl.when(jnp.logical_not(inside(me + offset)))
        def _():
            rows = pl.ds(slot * SUB, SUB)
            far_k[rows, :] = jnp.zeros((SUB, width), far_k.dtype)
            far_v[rows, :] = jnp.zeros((SUB, width), far_v.dtype)

    reach = jnp.broadcast_to(win[0], (tokens, tokens))
    query_row = lax.broadcasted_iota(jnp.int32, (tokens, tokens), 0) // COLS
    key_row = lax.broadcasted_iota(jnp.int32, (tokens, tokens), 1) // COLS
    bias[...] = jnp.where(jnp.abs(query_row - key_row) <= reach, 0.0, NEG)
    loads[2].wait()

    def update(head, tile, key, value, shift, first, last):
        columns = pl.ds(pl.multiple_of(head * HD, HD), HD)
        rows = pl.ds(tile * TILE, TILE)
        scores = lax.dot_general(
            qs[rows, columns], key, (((1,), (1,)), ((), ())), preferred_element_type=jnp.float32
        )
        if shift is not None:
            scores = scores + shift
        lanes = scores.shape[1] // HD
        high = jnp.broadcast_to(jnp.max(scores, axis=1, keepdims=True), (TILE, HD))
        if not first:
            old = peak[head, rows, :]
            high = jnp.maximum(old, high)
            fade = jnp.exp2((old - high) * FACTOR)
        raw = jnp.exp2((scores - jnp.concatenate([high] * lanes, axis=1)) * FACTOR)
        summed = raw[:, :HD]
        for lane in range(1, lanes):
            summed = summed + raw[:, lane * HD:(lane + 1) * HD]
        weighted = jnp.dot(raw.astype(jnp.bfloat16), value, preferred_element_type=jnp.float32)
        if not first:
            summed = summed + fade * total[head, rows, :]
            weighted = weighted + fade * acc[rows, columns]
        if last:
            row_total = jnp.sum(summed, axis=1, keepdims=True)
            out_ref[0, rows, columns] = (weighted / row_total).astype(out_ref.dtype)
        else:
            peak[head, rows, :] = high
            total[head, rows, :] = summed
            acc[rows, columns] = weighted

    def sweep(low, high, keys, values, shift_for, first=False, last=False):
        def one_head(head, carry):
            columns = pl.ds(pl.multiple_of(head * HD, HD), HD)
            key, value = keys(columns), values(columns)
            for tile in range(tokens // TILE):
                update(head, tile, key, value, shift_for(tile), first, last)
            return carry
        lax.fori_loop(low, high, one_head, 0)

    def near_bias(tile):
        return bias[pl.ds(tile * TILE, TILE), :]

    sweep(0, heads, lambda c: ks[:, c], lambda c: vs[:, c], near_bias, first=True)

    for chunk in range(CHUNKS):
        for side in range(2):
            @pl.when(inside(me - 1 if side == 0 else me + 1))
            def _():
                near_copy(side, chunk, 0).wait_recv()
                near_copy(side, chunk, 1).wait_recv()
                sweep(
                    chunk * part_heads, (chunk + 1) * part_heads,
                    lambda c: near_k[side, :, c], lambda c: near_v[side, :, c], near_bias,
                )

    def far_valid(offsets):
        pieces = [
            jnp.full((1, SUB), jnp.where(inside(me + offset), 0.0, NEG), jnp.float32)
            for offset in offsets
        ]
        return jnp.concatenate(pieces, axis=1)

    for slot, offset in enumerate(far_offsets):
        @pl.when(inside(me + offset))
        def _():
            far_copy(slot, offset, 0).wait_recv()
            far_copy(slot, offset, 1).wait_recv()
    far_copy(long_slot, steps[2], 0).wait_recv()
    far_copy(long_slot, steps[2], 1).wait_recv()
    shift = jnp.concatenate([far_valid(far_offsets), jnp.zeros((1, SUB), jnp.float32)], axis=1)
    sweep(0, heads, lambda c: far_k[:, c], lambda c: far_v[:, c], lambda tile: shift, last=True)

    each_near(lambda copy: copy.wait_send())
    for slot, offset, column in sends:
        @pl.when(inside(me - offset))
        def _():
            far_copy(slot, offset, 0).wait_send()
            far_copy(slot, offset, 1).wait_send()


def body(query_in, keys_in, values_in, far_picks, win_rows):
    frames = lax.axis_size("frame")
    _, tokens, width = query_in.shape
    heads = width // HD
    kind = query_in.dtype
    slots = 5 * SUB
    return pl.pallas_call(
        functools.partial(kernel, frames),
        out_shape=jax.ShapeDtypeStruct(query_in.shape, query_in.dtype),
        in_specs=[pl.BlockSpec(memory_space=pl.ANY)] * 3
        + [pl.BlockSpec(memory_space=pltpu.SMEM)] * 2,
        out_specs=pl.BlockSpec(memory_space=pltpu.VMEM),
        scratch_shapes=[
            pltpu.VMEM((tokens, width), kind),
            pltpu.VMEM((tokens, width), kind),
            pltpu.VMEM((tokens, width), kind),
            pltpu.VMEM((2, tokens, width), kind),
            pltpu.VMEM((2, tokens, width), kind),
            pltpu.VMEM((slots, width), kind),
            pltpu.VMEM((slots, width), kind),
            pltpu.VMEM((slots, width), kind),
            pltpu.VMEM((slots, width), kind),
            pltpu.VMEM((heads, tokens, HD), jnp.float32),
            pltpu.VMEM((heads, tokens, HD), jnp.float32),
            pltpu.VMEM((tokens, width), jnp.float32),
            pltpu.VMEM((tokens, tokens), jnp.float32),
            pltpu.SemaphoreType.DMA((3,)),
            pltpu.SemaphoreType.DMA((2, CHUNKS, 2)),
            pltpu.SemaphoreType.DMA((2, CHUNKS, 2)),
            pltpu.SemaphoreType.DMA((5, 2)),
            pltpu.SemaphoreType.DMA((5, 2)),
        ],
        compiler_params=pltpu.CompilerParams(
            collective_id=0, has_side_effects=True, vmem_limit_bytes=56 * 2**20
        ),
        cost_estimate=pl.CostEstimate(
            flops=4 * tokens * (3 * tokens + slots) * width,
            bytes_accessed=8 * tokens * width,
            transcendentals=heads * tokens * (3 * tokens + slots),
        ),
    )(query_in, keys_in, values_in, far_picks, win_rows)


def solution(mesh):
    in_specs = (
        P(("groups", "frame"), None, None),
        P(("groups", "frame"), None, None),
        P(("groups", "frame"), None, None),
        P("groups", None),
        P(("groups", "frame")),
    )
    out_specs = P(("groups", "frame"), None, None)
    return jax.shard_map(body, mesh=mesh, in_specs=in_specs, out_specs=out_specs, check_vma=False)
```

```python
import functools
import math

import jax
import jax.numpy as jnp
from jax import lax
from jax.experimental import pallas as pl
from jax.experimental.pallas import tpu as pltpu
from jax.sharding import PartitionSpec as P

HD = 128
COLS = 32
SUB = 128
NREACH = 3
NEG = -1e30
CHUNKS = 3
TILE = 256
FACTOR = math.log2(math.e) / math.sqrt(HD)


def kernel(
    frames, q_hbm, k_hbm, v_hbm, picks, win, out_ref,
    qs, ks, vs, mate_k, mate_v, ext_k, ext_v, relay_k, relay_v,
    stage_k, stage_v, far_k, far_v,
    peak, total, acc, bias,
    in_sem, mate_send, mate_recv, ext_send, ext_recv, relay_send, relay_recv,
    far_send, far_recv, via_send, via_recv,
):
    tokens, width = qs.shape
    heads = width // HD
    part = width // CHUNKS
    part_heads = heads // CHUNKS
    units = 2 * CHUNKS
    group = lax.axis_index("groups")
    me = lax.axis_index("frame")
    steps = [frames // 2 ** (NREACH - j) for j in range(NREACH)]
    via_mate = steps[0] == 2
    quads = frames // 4 if frames % 4 == 0 else 0

    def inside(index):
        return (index >= 0) & (index < frames)

    odd = me % 2
    side = 2 * odd - 1
    mate = me - side
    outer = me + side
    has_outer = inside(outer)

    def relayed(sender):
        span = max(quads, 1)
        low = jnp.where(odd == 1, sender // 4, sender // 4 - 1)
        weight = jnp.where(odd == 1, span - 1 - low, low + 1)
        return jnp.minimum(units, (15 * weight + span) // (2 * span))

    place = me % 4
    if quads:
        crossing = ((place == 0) | (place == 3)) & has_outer
        is_relay = ((place == 1) | (place == 2)) & inside(me + 3 * side)
        my_relayed = jnp.where(crossing, relayed(me), 0)
        to_relay = jnp.where(is_relay, relayed(me + 2 * side), 0)
    else:
        crossing = place < 0
        my_relayed = to_relay = jnp.int32(0)

    loads = [
        pltpu.make_async_copy(src, dst, in_sem.at[i])
        for i, (src, dst) in enumerate(((k_hbm.at[0], ks), (v_hbm.at[0], vs), (q_hbm.at[0], qs)))
    ]
    for load in loads:
        load.start()

    barrier = pltpu.get_barrier_semaphore()
    count = jnp.int32(0)
    for distance in sorted({1, 2, 3, *steps}):
        for offset in (-distance, distance):
            ok = inside(me + offset)
            count = count + ok.astype(jnp.int32)

            @pl.when(ok)
            def _():
                pl.semaphore_signal(
                    barrier, inc=1, device_id=(group, me + offset),
                    device_id_type=pl.DeviceIdType.MESH,
                )
    pl.semaphore_wait(barrier, count)

    def remote(src, dst, send, recv, target):
        return pltpu.make_async_remote_copy(
            src_ref=src, dst_ref=dst, send_sem=send, recv_sem=recv,
            device_id=(group, target), device_id_type=pl.DeviceIdType.MESH,
        )

    def piece(unit):
        return pl.ds((unit // 2) * part, part)

    def mate_copy(unit):
        return remote(
            (k_hbm, v_hbm)[unit % 2].at[0, :, piece(unit)],
            (mate_k, mate_v)[unit % 2].at[:, piece(unit)],
            mate_send.at[unit], mate_recv.at[unit], mate,
        )

    def ext_copy(unit):
        return remote(
            (k_hbm, v_hbm)[unit % 2].at[0, :, piece(unit)],
            (ext_k, ext_v)[unit % 2].at[:, piece(unit)],
            ext_send.at[unit], ext_recv.at[unit], outer,
        )

    def to_relay_copy(unit):
        return remote(
            (k_hbm, v_hbm)[unit % 2].at[0, :, piece(unit)],
            (relay_k, relay_v)[unit % 2].at[:, piece(unit)],
            ext_send.at[unit], relay_recv.at[unit], me - 2 * side,
        )

    def relay_copy(unit):
        return remote(
            (relay_k, relay_v)[unit % 2].at[:, piece(unit)],
            (ext_k, ext_v)[unit % 2].at[:, piece(unit)],
            relay_send.at[unit], ext_recv.at[unit], me + 3 * side,
        )

    def far_copy(slot, target, kind):
        rows = pl.ds(slot * SUB, SUB)
        return remote(
            (stage_k, stage_v)[kind].at[rows, :], (far_k, far_v)[kind].at[rows, :],
            far_send.at[slot, kind], far_recv.at[slot, kind], target,
        )

    def via_copy(unit):
        rows = pl.ds(SUB, SUB)
        return remote(
            (stage_k, stage_v)[unit % 2].at[rows, piece(unit)],
            (far_k, far_v)[unit % 2].at[rows, piece(unit)],
            via_send.at[unit], via_recv.at[unit], mate,
        )

    def stage(slot, pick, src_k, src_v, low, high):
        chosen = jnp.broadcast_to(pick, (16, HD))
        hot = [
            jnp.concatenate(
                [jnp.where(chosen == block, 1.0, 0.0).astype(stage_k.dtype)] * (SUB // 16), axis=0
            )
            for block in range(tokens // SUB)
        ]

        def one_head(head, carry):
            columns = pl.ds(pl.multiple_of(head * HD, HD), HD)
            for src, dst in ((src_k, stage_k), (src_v, stage_v)):
                mixed = hot[0] * src[pl.ds(0, SUB), columns]
                for block in range(1, tokens // SUB):
                    mixed = mixed + hot[block] * src[pl.ds(block * SUB, SUB), columns]
                dst[pl.ds(slot * SUB, SUB), columns] = mixed
            return carry
        lax.fori_loop(low, high, one_head, 0)

    long_sends = [
        (4, me + steps[2], NREACH - 1), (4, me - steps[2], 2 * NREACH - 1),
        (2, me + steps[1], 1), (3, me - steps[1], NREACH + 1),
    ]
    short_sends = [(0, me - steps[0] * side, NREACH * odd)]
    if not via_mate:
        short_sends.append((1, me + steps[0] * side, NREACH * (1 - odd)))
    long_sources = [(2, me - steps[1]), (3, me + steps[1])]
    short_sources = [(0, me + steps[0] * side), (1, me - steps[0] * side)]

    def send_far(sends):
        for slot, reader, column in sends:
            @pl.when(inside(reader))
            def _():
                stage(slot, picks[reader, column], ks, vs, 0, heads)
                far_copy(slot, reader, 0).start()
                far_copy(slot, reader, 1).start()

    for unit in range(units):
        @pl.when(crossing & (unit < my_relayed))
        def _():
            to_relay_copy(unit).start()

        @pl.when(crossing & (unit >= my_relayed))
        def _():
            ext_copy(unit).start()
    for unit in range(units):
        mate_copy(unit).start()

    loads[0].wait()
    loads[1].wait()
    send_far(long_sends)

    for slot, source in long_sources + short_sources:
        @pl.when(jnp.logical_not(inside(source)))
        def _():
            rows = pl.ds(slot * SUB, SUB)
            far_k[rows, :] = jnp.zeros((SUB, width), far_k.dtype)
            far_v[rows, :] = jnp.zeros((SUB, width), far_v.dtype)

    reach = jnp.broadcast_to(win[0], (tokens, tokens))
    query_row = lax.broadcasted_iota(jnp.int32, (tokens, tokens), 0) // COLS
    key_row = lax.broadcasted_iota(jnp.int32, (tokens, tokens), 1) // COLS
    bias[...] = jnp.where(jnp.abs(query_row - key_row) <= reach, 0.0, NEG)
    loads[2].wait()

    def update(head, tile, key, value, shift, first, last):
        columns = pl.ds(pl.multiple_of(head * HD, HD), HD)
        rows = pl.ds(tile * TILE, TILE)
        scores = lax.dot_general(
            qs[rows, columns], key, (((1,), (1,)), ((), ())), preferred_element_type=jnp.float32
        )
        if shift is not None:
            scores = scores + shift
        lanes = scores.shape[1] // HD
        high = jnp.broadcast_to(jnp.max(scores, axis=1, keepdims=True), (TILE, HD))
        if not first:
            old = peak[head, rows, :]
            high = jnp.maximum(old, high)
            fade = jnp.exp2((old - high) * FACTOR)
        raw = jnp.exp2((scores - jnp.concatenate([high] * lanes, axis=1)) * FACTOR)
        summed = raw[:, :HD]
        for lane in range(1, lanes):
            summed = summed + raw[:, lane * HD:(lane + 1) * HD]
        weighted = jnp.dot(raw.astype(jnp.bfloat16), value, preferred_element_type=jnp.float32)
        if not first:
            summed = summed + fade * total[head, rows, :]
            weighted = weighted + fade * acc[rows, columns]
        if last:
            row_total = jnp.sum(summed, axis=1, keepdims=True)
            out_ref[0, rows, columns] = (weighted / row_total).astype(out_ref.dtype)
        else:
            peak[head, rows, :] = high
            total[head, rows, :] = summed
            acc[rows, columns] = weighted

    def sweep(low, high, keys, values, shift_for, first=False, last=False):
        def one_head(head, carry):
            columns = pl.ds(pl.multiple_of(head * HD, HD), HD)
            key, value = keys(columns), values(columns)
            for tile in range(tokens // TILE):
                update(head, tile, key, value, shift_for(tile), first, last)
            return carry
        lax.fori_loop(low, high, one_head, 0)

    def near_bias(tile):
        return bias[pl.ds(tile * TILE, TILE), :]

    def start_direct():
        send_far(short_sends)
        for unit in range(units):
            @pl.when(has_outer & jnp.logical_not(crossing))
            def _():
                ext_copy(unit).start()

    def pass_on(unit):
        @pl.when(unit < to_relay)
        def _():
            to_relay_copy(unit).wait_recv()
            relay_copy(unit).start()

    def far_shift(sources):
        pieces = [
            jnp.full((1, SUB), jnp.where(inside(source), 0.0, NEG), jnp.float32)
            for _, source in sources
        ]
        return jnp.concatenate(pieces, axis=1)

    sweep(0, heads, lambda c: ks[:, c], lambda c: vs[:, c], near_bias, first=True)
    pass_on(0)
    for chunk in range(CHUNKS):
        mate_copy(2 * chunk).wait_recv()
        mate_copy(2 * chunk + 1).wait_recv()
        sweep(
            chunk * part_heads, (chunk + 1) * part_heads,
            lambda c: mate_k[:, c], lambda c: mate_v[:, c], near_bias,
        )
        if chunk == 0:
            start_direct()
        pass_on(chunk + 1)

    for slot, source in long_sources:
        @pl.when(inside(source))
        def _():
            far_copy(slot, me, 0).wait_recv()
            far_copy(slot, me, 1).wait_recv()
    far_copy(4, me, 0).wait_recv()
    far_copy(4, me, 1).wait_recv()
    long_shift = jnp.concatenate([far_shift(long_sources), jnp.zeros((1, SUB), jnp.float32)], axis=1)
    long_rows = pl.ds(2 * SUB, 3 * SUB)
    sweep(0, heads, lambda c: far_k[long_rows, c], lambda c: far_v[long_rows, c], lambda tile: long_shift)
    for unit in range(CHUNKS + 1, units):
        pass_on(unit)

    short_shift = far_shift(short_sources)
    short_rows = pl.ds(0, 2 * SUB)
    for slot, source in short_sources[:1] if via_mate else short_sources:
        @pl.when(inside(source))
        def _():
            far_copy(slot, me, 0).wait_recv()
            far_copy(slot, me, 1).wait_recv()
    for chunk in range(CHUNKS):
        low, high = chunk * part_heads, (chunk + 1) * part_heads

        @pl.when(has_outer)
        def _():
            ext_copy(2 * chunk).wait_recv()
            ext_copy(2 * chunk + 1).wait_recv()
            if via_mate:
                stage(1, picks[mate, NREACH * odd], ext_k, ext_v, low, high)
                via_copy(2 * chunk).start()
                via_copy(2 * chunk + 1).start()
            sweep(low, high, lambda c: ext_k[:, c], lambda c: ext_v[:, c], near_bias)

        if via_mate:
            @pl.when(inside(me - 2 * side))
            def _():
                via_copy(2 * chunk).wait_recv()
                via_copy(2 * chunk + 1).wait_recv()
        sweep(
            low, high, lambda c: far_k[short_rows, c], lambda c: far_v[short_rows, c],
            lambda tile: short_shift, last=True,
        )

    for unit in range(units):
        mate_copy(unit).wait_send()

        @pl.when(has_outer)
        def _():
            ext_copy(unit).wait_send()
            if via_mate:
                via_copy(unit).wait_send()

        @pl.when(unit < to_relay)
        def _():
            relay_copy(unit).wait_send()
    for slot, reader, column in long_sends + short_sends:
        @pl.when(inside(reader))
        def _():
            far_copy(slot, reader, 0).wait_send()
            far_copy(slot, reader, 1).wait_send()


def body(query_in, keys_in, values_in, far_picks, win_rows):
    frames = lax.axis_size("frame")
    _, tokens, width = query_in.shape
    heads = width // HD
    kind = query_in.dtype
    slots = 5 * SUB
    return pl.pallas_call(
        functools.partial(kernel, frames),
        out_shape=jax.ShapeDtypeStruct(query_in.shape, query_in.dtype),
        in_specs=[pl.BlockSpec(memory_space=pl.ANY)] * 3
        + [pl.BlockSpec(memory_space=pltpu.SMEM)] * 2,
        out_specs=pl.BlockSpec(memory_space=pltpu.VMEM),
        scratch_shapes=[pltpu.VMEM((tokens, width), kind)] * 9
        + [pltpu.VMEM((slots, width), kind)] * 4
        + [pltpu.VMEM((heads, tokens, HD), jnp.float32)] * 2
        + [pltpu.VMEM((tokens, width), jnp.float32), pltpu.VMEM((tokens, tokens), jnp.float32)]
        + [pltpu.SemaphoreType.DMA((3,))]
        + [pltpu.SemaphoreType.DMA((2 * CHUNKS,))] * 6
        + [pltpu.SemaphoreType.DMA((5, 2))] * 2
        + [pltpu.SemaphoreType.DMA((2 * CHUNKS,))] * 2,
        compiler_params=pltpu.CompilerParams(
            collective_id=0, has_side_effects=True, vmem_limit_bytes=56 * 2**20
        ),
        cost_estimate=pl.CostEstimate(
            flops=4 * tokens * (3 * tokens + slots) * width,
            bytes_accessed=8 * tokens * width,
            transcendentals=heads * tokens * (3 * tokens + slots),
        ),
    )(query_in, keys_in, values_in, far_picks, win_rows)


def solution(mesh):
    in_specs = (
        P(("groups", "frame"), None, None),
        P(("groups", "frame"), None, None),
        P(("groups", "frame"), None, None),
        P("groups", None),
        P(("groups", "frame")),
    )
    out_specs = P(("groups", "frame"), None, None)
    return jax.shard_map(body, mesh=mesh, in_specs=in_specs, out_specs=out_specs, check_vma=False)
```

```python
import functools
import math

import jax
import jax.numpy as jnp
from jax import lax
from jax.experimental import pallas as pl
from jax.experimental.pallas import tpu as pltpu
from jax.sharding import PartitionSpec as P

HD = 128
COLS = 32
SUB = 128
NREACH = 3
NEG = -1e30
CHUNKS = 3
TILE = 256
FACTOR = math.log2(math.e) / math.sqrt(HD)


def kernel(
    frames, q_hbm, k_hbm, v_hbm, picks, win, out_ref,
    qs, ks, vs, mate_k, mate_v, ext_k, ext_v, relay_k, relay_v,
    stage_k, stage_v, far_k, far_v,
    peak, total, acc, bias,
    in_sem, mate_send, mate_recv, ext_send, ext_recv, relay_send, relay_recv,
    far_send, far_recv, via_send, via_recv,
):
    tokens, width = qs.shape
    heads = width // HD
    part = width // CHUNKS
    part_heads = heads // CHUNKS
    units = 2 * CHUNKS
    group = lax.axis_index("groups")
    me = lax.axis_index("frame")
    steps = [frames // 2 ** (NREACH - j) for j in range(NREACH)]
    via_mate = steps[0] == 2
    quads = frames // 4 if frames % 4 == 0 else 0

    def inside(index):
        return (index >= 0) & (index < frames)

    odd = me % 2
    side = 2 * odd - 1
    mate = me - side
    outer = me + side
    has_outer = inside(outer)

    def relayed(sender):
        span = max(quads, 1)
        low = jnp.where(odd == 1, sender // 4, sender // 4 - 1)
        weight = jnp.where(odd == 1, span - 1 - low, low + 1)
        return jnp.minimum(units, (15 * weight + span) // (2 * span))

    place = me % 4
    if quads:
        crossing = ((place == 0) | (place == 3)) & has_outer
        is_relay = ((place == 1) | (place == 2)) & inside(me + 3 * side)
        my_relayed = jnp.where(crossing, relayed(me), 0)
        to_relay = jnp.where(is_relay, relayed(me + 2 * side), 0)
    else:
        crossing = place < 0
        my_relayed = to_relay = jnp.int32(0)

    loads = [
        pltpu.make_async_copy(src, dst, in_sem.at[i])
        for i, (src, dst) in enumerate(((k_hbm.at[0], ks), (v_hbm.at[0], vs), (q_hbm.at[0], qs)))
    ]
    for load in loads:
        load.start()

    barrier = pltpu.get_barrier_semaphore()
    count = jnp.int32(0)
    for distance in sorted({1, 2, 3, *steps}):
        for offset in (-distance, distance):
            ok = inside(me + offset)
            count = count + ok.astype(jnp.int32)

            @pl.when(ok)
            def _():
                pl.semaphore_signal(
                    barrier, inc=1, device_id=(group, me + offset),
                    device_id_type=pl.DeviceIdType.MESH,
                )
    pl.semaphore_wait(barrier, count)

    def remote(src, dst, send, recv, target):
        return pltpu.make_async_remote_copy(
            src_ref=src, dst_ref=dst, send_sem=send, recv_sem=recv,
            device_id=(group, target), device_id_type=pl.DeviceIdType.MESH,
        )

    def piece(unit):
        return pl.ds((unit // 2) * part, part)

    def mate_copy(unit):
        return remote(
            (k_hbm, v_hbm)[unit % 2].at[0, :, piece(unit)],
            (mate_k, mate_v)[unit % 2].at[:, piece(unit)],
            mate_send.at[unit], mate_recv.at[unit], mate,
        )

    def ext_copy(unit):
        return remote(
            (k_hbm, v_hbm)[unit % 2].at[0, :, piece(unit)],
            (ext_k, ext_v)[unit % 2].at[:, piece(unit)],
            ext_send.at[unit], ext_recv.at[unit], outer,
        )

    def to_relay_copy(unit):
        return remote(
            (k_hbm, v_hbm)[unit % 2].at[0, :, piece(unit)],
            (relay_k, relay_v)[unit % 2].at[:, piece(unit)],
            ext_send.at[unit], relay_recv.at[unit], me - 2 * side,
        )

    def relay_copy(unit):
        return remote(
            (relay_k, relay_v)[unit % 2].at[:, piece(unit)],
            (ext_k, ext_v)[unit % 2].at[:, piece(unit)],
            relay_send.at[unit], ext_recv.at[unit], me + 3 * side,
        )

    def far_copy(slot, target, kind):
        rows = pl.ds(slot * SUB, SUB)
        return remote(
            (stage_k, stage_v)[kind].at[rows, :], (far_k, far_v)[kind].at[rows, :],
            far_send.at[slot, kind], far_recv.at[slot, kind], target,
        )

    def via_copy(unit):
        rows = pl.ds(SUB, SUB)
        return remote(
            (stage_k, stage_v)[unit % 2].at[rows, piece(unit)],
            (far_k, far_v)[unit % 2].at[rows, piece(unit)],
            via_send.at[unit], via_recv.at[unit], mate,
        )

    def stage(slot, pick, src_k, src_v, low, high):
        chosen = jnp.broadcast_to(pick, (16, HD))
        hot = [
            jnp.concatenate(
                [jnp.where(chosen == block, 1.0, 0.0).astype(stage_k.dtype)] * (SUB // 16), axis=0
            )
            for block in range(tokens // SUB)
        ]

        def one_head(head, carry):
            columns = pl.ds(pl.multiple_of(head * HD, HD), HD)
            for src, dst in ((src_k, stage_k), (src_v, stage_v)):
                mixed = hot[0] * src[pl.ds(0, SUB), columns]
                for block in range(1, tokens // SUB):
                    mixed = mixed + hot[block] * src[pl.ds(block * SUB, SUB), columns]
                dst[pl.ds(slot * SUB, SUB), columns] = mixed
            return carry
        lax.fori_loop(low, high, one_head, 0)

    long_sends = [
        (4, me + steps[2], NREACH - 1), (4, me - steps[2], 2 * NREACH - 1),
        (2, me + steps[1], 1), (3, me - steps[1], NREACH + 1),
    ]
    short_sends = [(0, me - steps[0] * side, NREACH * odd)]
    if not via_mate:
        short_sends.append((1, me + steps[0] * side, NREACH * (1 - odd)))
    long_sources = [(2, me - steps[1]), (3, me + steps[1])]
    short_sources = [(0, me + steps[0] * side), (1, me - steps[0] * side)]

    def send_far(sends):
        for slot, reader, column in sends:
            @pl.when(inside(reader))
            def _():
                stage(slot, picks[reader, column], ks, vs, 0, heads)
                far_copy(slot, reader, 0).start()
                far_copy(slot, reader, 1).start()

    def start_crossing(chunk):
        for unit in (2 * chunk, 2 * chunk + 1):
            @pl.when(crossing & (unit < my_relayed))
            def _():
                to_relay_copy(unit).start()

            @pl.when(crossing & (unit >= my_relayed))
            def _():
                ext_copy(unit).start()

    start_crossing(0)
    for unit in range(units):
        mate_copy(unit).start()

    loads[0].wait()
    loads[1].wait()
    send_far(long_sends)

    for slot, source in long_sources + short_sources:
        @pl.when(jnp.logical_not(inside(source)))
        def _():
            rows = pl.ds(slot * SUB, SUB)
            far_k[rows, :] = jnp.zeros((SUB, width), far_k.dtype)
            far_v[rows, :] = jnp.zeros((SUB, width), far_v.dtype)

    reach = jnp.broadcast_to(win[0], (tokens, tokens))
    query_row = lax.broadcasted_iota(jnp.int32, (tokens, tokens), 0) // COLS
    key_row = lax.broadcasted_iota(jnp.int32, (tokens, tokens), 1) // COLS
    bias[...] = jnp.where(jnp.abs(query_row - key_row) <= reach, 0.0, NEG)
    loads[2].wait()

    def update(head, tile, key, value, shift, first, last):
        columns = pl.ds(pl.multiple_of(head * HD, HD), HD)
        rows = pl.ds(tile * TILE, TILE)
        scores = lax.dot_general(
            qs[rows, columns], key, (((1,), (1,)), ((), ())), preferred_element_type=jnp.float32
        )
        if shift is not None:
            scores = scores + shift
        lanes = scores.shape[1] // HD
        high = jnp.broadcast_to(jnp.max(scores, axis=1, keepdims=True), (TILE, HD))
        if not first:
            old = peak[head, rows, :]
            high = jnp.maximum(old, high)
            fade = jnp.exp2((old - high) * FACTOR)
        raw = jnp.exp2((scores - jnp.concatenate([high] * lanes, axis=1)) * FACTOR)
        summed = raw[:, :HD]
        for lane in range(1, lanes):
            summed = summed + raw[:, lane * HD:(lane + 1) * HD]
        weighted = jnp.dot(raw.astype(jnp.bfloat16), value, preferred_element_type=jnp.float32)
        if not first:
            summed = summed + fade * total[head, rows, :]
            weighted = weighted + fade * acc[rows, columns]
        if last:
            row_total = jnp.sum(summed, axis=1, keepdims=True)
            out_ref[0, rows, columns] = (weighted / row_total).astype(out_ref.dtype)
        else:
            peak[head, rows, :] = high
            total[head, rows, :] = summed
            acc[rows, columns] = weighted

    def sweep(low, high, keys, values, shift_for, first=False, last=False):
        def one_head(head, carry):
            columns = pl.ds(pl.multiple_of(head * HD, HD), HD)
            key, value = keys(columns), values(columns)
            for tile in range(tokens // TILE):
                update(head, tile, key, value, shift_for(tile), first, last)
            return carry
        lax.fori_loop(low, high, one_head, 0)

    def near_bias(tile):
        return bias[pl.ds(tile * TILE, TILE), :]

    def start_direct(chunk):
        for unit in (2 * chunk, 2 * chunk + 1):
            @pl.when(has_outer & jnp.logical_not(crossing))
            def _():
                ext_copy(unit).start()

    def pass_on(unit):
        @pl.when(unit < to_relay)
        def _():
            to_relay_copy(unit).wait_recv()
            relay_copy(unit).start()

    def far_shift(sources):
        pieces = [
            jnp.full((1, SUB), jnp.where(inside(source), 0.0, NEG), jnp.float32)
            for _, source in sources
        ]
        return jnp.concatenate(pieces, axis=1)

    sweep(0, 2 * part_heads, lambda c: ks[:, c], lambda c: vs[:, c], near_bias, first=True)
    start_crossing(1)
    sweep(2 * part_heads, heads, lambda c: ks[:, c], lambda c: vs[:, c], near_bias, first=True)
    send_far(short_sends)
    start_direct(0)
    pass_on(0)
    for chunk in range(CHUNKS):
        mate_copy(2 * chunk).wait_recv()
        mate_copy(2 * chunk + 1).wait_recv()
        sweep(
            chunk * part_heads, (chunk + 1) * part_heads,
            lambda c: mate_k[:, c], lambda c: mate_v[:, c], near_bias,
        )
        if chunk == 0:
            start_crossing(2)
            start_direct(1)
        if chunk == 2:
            start_direct(2)
        pass_on(chunk + 1)

    for slot, source in long_sources:
        @pl.when(inside(source))
        def _():
            far_copy(slot, me, 0).wait_recv()
            far_copy(slot, me, 1).wait_recv()
    far_copy(4, me, 0).wait_recv()
    far_copy(4, me, 1).wait_recv()
    long_shift = jnp.concatenate([far_shift(long_sources), jnp.zeros((1, SUB), jnp.float32)], axis=1)
    long_rows = pl.ds(2 * SUB, 3 * SUB)
    sweep(0, heads, lambda c: far_k[long_rows, c], lambda c: far_v[long_rows, c], lambda tile: long_shift)
    for unit in range(CHUNKS + 1, units):
        pass_on(unit)

    short_shift = far_shift(short_sources)
    short_rows = pl.ds(0, 2 * SUB)
    for slot, source in short_sources[:1] if via_mate else short_sources:
        @pl.when(inside(source))
        def _():
            far_copy(slot, me, 0).wait_recv()
            far_copy(slot, me, 1).wait_recv()
    for chunk in range(CHUNKS):
        low, high = chunk * part_heads, (chunk + 1) * part_heads

        @pl.when(has_outer)
        def _():
            ext_copy(2 * chunk).wait_recv()
            ext_copy(2 * chunk + 1).wait_recv()
            if via_mate:
                stage(1, picks[mate, NREACH * odd], ext_k, ext_v, low, high)
                via_copy(2 * chunk).start()
                via_copy(2 * chunk + 1).start()
            sweep(low, high, lambda c: ext_k[:, c], lambda c: ext_v[:, c], near_bias)

        if via_mate:
            @pl.when(inside(me - 2 * side))
            def _():
                via_copy(2 * chunk).wait_recv()
                via_copy(2 * chunk + 1).wait_recv()
        sweep(
            low, high, lambda c: far_k[short_rows, c], lambda c: far_v[short_rows, c],
            lambda tile: short_shift, last=True,
        )

    for unit in range(units):
        mate_copy(unit).wait_send()

        @pl.when(has_outer)
        def _():
            ext_copy(unit).wait_send()
            if via_mate:
                via_copy(unit).wait_send()

        @pl.when(unit < to_relay)
        def _():
            relay_copy(unit).wait_send()
    for slot, reader, column in long_sends + short_sends:
        @pl.when(inside(reader))
        def _():
            far_copy(slot, reader, 0).wait_send()
            far_copy(slot, reader, 1).wait_send()


def body(query_in, keys_in, values_in, far_picks, win_rows):
    frames = lax.axis_size("frame")
    _, tokens, width = query_in.shape
    heads = width // HD
    kind = query_in.dtype
    slots = 5 * SUB
    return pl.pallas_call(
        functools.partial(kernel, frames),
        out_shape=jax.ShapeDtypeStruct(query_in.shape, query_in.dtype),
        in_specs=[pl.BlockSpec(memory_space=pl.ANY)] * 3
        + [pl.BlockSpec(memory_space=pltpu.SMEM)] * 2,
        out_specs=pl.BlockSpec(memory_space=pltpu.VMEM),
        scratch_shapes=[pltpu.VMEM((tokens, width), kind)] * 9
        + [pltpu.VMEM((slots, width), kind)] * 4
        + [pltpu.VMEM((heads, tokens, HD), jnp.float32)] * 2
        + [pltpu.VMEM((tokens, width), jnp.float32), pltpu.VMEM((tokens, tokens), jnp.float32)]
        + [pltpu.SemaphoreType.DMA((3,))]
        + [pltpu.SemaphoreType.DMA((2 * CHUNKS,))] * 6
        + [pltpu.SemaphoreType.DMA((5, 2))] * 2
        + [pltpu.SemaphoreType.DMA((2 * CHUNKS,))] * 2,
        compiler_params=pltpu.CompilerParams(
            collective_id=0, has_side_effects=True, vmem_limit_bytes=56 * 2**20
        ),
        cost_estimate=pl.CostEstimate(
            flops=4 * tokens * (3 * tokens + slots) * width,
            bytes_accessed=8 * tokens * width,
            transcendentals=heads * tokens * (3 * tokens + slots),
        ),
    )(query_in, keys_in, values_in, far_picks, win_rows)


def solution(mesh):
    in_specs = (
        P(("groups", "frame"), None, None),
        P(("groups", "frame"), None, None),
        P(("groups", "frame"), None, None),
        P("groups", None),
        P(("groups", "frame")),
    )
    out_specs = P(("groups", "frame"), None, None)
    return jax.shard_map(body, mesh=mesh, in_specs=in_specs, out_specs=out_specs, check_vma=False)
```
